128 devices in a mesh: section: 32 (over y, x, core), expert: 4 (over z).
Axes of the slice: x: 4, y: 4, z: 4, core: 2. Of those that a mesh axis runs over, the one named last changes fastest.
Arguments:
- tokens: bfloat16 [65536, 2880], P(('section', 'expert')), may hold values from -6 to 6
- segment_norm_scale: float32 [32, 2880], P('section'), may hold values from 0.1 to 1.9
- expert_choice_table: int32 [4, 65536, 4], P(None, ('section', 'expert')), may hold values from 0 to 127, as said below
- router_weight_table: bfloat16 [4, 65536, 4], P(None, ('section', 'expert')), may hold values from 0.099609375 to 1
- adapter_down_weight: bfloat16 [32, 2880, 128], P('section'), may hold values from -0.109375 to 0.109375
- adapter_up_weight: bfloat16 [32, 128, 2880], P('section'), may hold values from -0.5 to 0.5
- expert_gate_up_weight: bfloat16 [32, 2880, 2, 1440], P('section', None, None, 'expert'), may hold values from -0.109375 to 0.109375
- expert_down_weight: bfloat16 [32, 1440, 2880], P('section', 'expert'), may hold values from -0.15625 to 0.15625
Outputs:
- carried: bfloat16 [65536, 2880], P(('section', 'expert'))
The draws below stay inside these ranges and needn't reach their ends.
Inputs may be any that keep to these rules, and one draw needn't show every extreme that they name: `expert_choice_table`: each row names 4 different experts. Within the rows of one device at one hop, at most 48 rows name expert 0, and in each hop some device has exactly 48 such rows.
All inputs are finite; a program needn't handle non-finite values.
Results may differ from the reference program's by a relative error of at most 0.014.
Values may be sent and summed in bfloat16 or wider, within the bound.
No kernel may reach another device: no remote copies, remote signals or barrier semaphores. Data moves between devices by JAX's collectives and lax.ppermute only.
A program may use at most 128 MiB of HBM per device.

```python
import math
import jax
import jax.numpy as jnp
from jax import lax

MODEL_WIDTH = 2880
EXPERTS = 128
HID = 1440
ADAPTER_RANK = 128
TOP = 4
CAP = 48
TOK_DEV = 512
HOPS = 4
TOKENS = 65536
N_SECTION = 32
N_EXPERT = 4


def draw_expert_choice_table(key, part):
    blocks = HOPS * (TOKENS // TOK_DEV)
    key_count, key_full, key_rank, key_base, key_place = jax.random.split(key, 5)
    counts = jax.random.randint(key_count, (blocks,), CAP // 2, CAP + 1)
    full_block = jax.random.randint(key_full, (HOPS,), 0, TOKENS // TOK_DEV)
    block_ids = jnp.arange(blocks, dtype=jnp.int32).reshape(HOPS, TOKENS // TOK_DEV) % (TOKENS // TOK_DEV)
    forced = (block_ids == full_block[:, None]).reshape(-1)
    counts = jnp.where(forced, CAP, counts)
    ranks = jax.vmap(lambda k: jax.random.permutation(k, TOK_DEV))(jax.random.split(key_rank, blocks))
    in_window = ranks < counts[:, None]
    base = jax.random.randint(key_base, (blocks, TOK_DEV, 1), 0, EXPERTS - 1)
    stride = (EXPERTS - 1) // TOP
    others = 1 + (base + stride * jnp.arange(TOP, dtype=jnp.int32)[None, None, :]) % (EXPERTS - 1)
    place = jax.random.randint(key_place, (blocks, TOK_DEV, 1), 0, TOP)
    hit = in_window[..., None] & (jnp.arange(TOP, dtype=jnp.int32)[None, None, :] == place)
    picks = jnp.where(hit, 0, others)
    return picks.reshape(HOPS, TOKENS, TOP).astype(jnp.int32)


def block_levels(key, shape, cuts, least, largest):
    gain = 1.0
    for dim, shards_of in cuts:
        steps = jax.random.uniform(jax.random.fold_in(jax.random.fold_in(key, 6), dim), (shards_of,), jnp.float32, least / len(cuts), largest / len(cuts))
        gain = gain * jnp.repeat(jnp.exp(steps), shape[dim] // shards_of).reshape((-1,) + (1,) * (len(shape) - 1 - dim))
    return gain


def noise(rng, shape, scale, limit, cuts=(), kind=jnp.bfloat16):
    entries = scale * jax.random.normal(rng, shape, jnp.float32)
    if cuts:
        entries = entries * block_levels(rng, shape, cuts, -0.22, 0.18)
    return jnp.clip(entries, -limit, limit).astype(kind)


def setup_inputs(seed: int = 0) -> dict:
    streams_of = jax.random.split(jax.random.key(seed), 9)
    tokens = noise(streams_of[0], (TOKENS, MODEL_WIDTH), 1.0, 6.0, ((0, 128),))
    segment_norm_scale = jnp.clip(1.0 + 0.18 * jax.random.normal(streams_of[1], (N_SECTION, MODEL_WIDTH), jnp.float32), 0.1, 1.9)
    expert_choice_table = draw_expert_choice_table(jax.random.fold_in(streams_of[8], 71), 0)
    router_weight_table = jnp.clip(jnp.exp(math.log(1.0) - 2.306499 * jax.random.uniform(streams_of[3], (HOPS, TOKENS, TOP), jnp.float32) ** block_levels(streams_of[3], (HOPS, TOKENS, TOP), ((1, 128),), -0.2, 0.2)), 0.099609375, 1.0).astype(jnp.bfloat16)
    adapter_down_weight = noise(streams_of[4], (N_SECTION, MODEL_WIDTH, ADAPTER_RANK), MODEL_WIDTH ** -0.5, 0.109375, ((0, 32),))
    adapter_up_weight = noise(streams_of[5], (N_SECTION, ADAPTER_RANK, MODEL_WIDTH), ADAPTER_RANK ** -0.5, 0.5, ((0, 32),))
    expert_gate_up_weight = noise(streams_of[6], (N_SECTION, MODEL_WIDTH, 2, HID), MODEL_WIDTH ** -0.5, 0.109375, ((0, 32), (3, 4)))
    expert_down_weight = noise(streams_of[7], (N_SECTION, HID, MODEL_WIDTH), HID ** -0.5, 0.15625, ((0, 32), (1, 4)))
    return {"tokens": tokens, "segment_norm_scale": segment_norm_scale, "expert_choice_table": expert_choice_table, "router_weight_table": router_weight_table, "adapter_down_weight": adapter_down_weight, "adapter_up_weight": adapter_up_weight, "expert_gate_up_weight": expert_gate_up_weight, "expert_down_weight": expert_down_weight}


def window_tables(expert_choice_rows, mix_row):
    flags = jnp.any(expert_choice_rows == 0, axis=-1)
    flag_int = flags.astype(jnp.int32)
    position = jnp.cumsum(flag_int) - flag_int
    slot_index = jnp.where(flags, position, CAP).astype(jnp.int32)
    select = (jnp.arange(CAP, dtype=jnp.int32)[:, None] == slot_index[None, :]).astype(jnp.bfloat16)
    mix_values = mix_row.astype(jnp.float32)
    chosen = lax.optimization_barrier(jnp.sum(jnp.where(expert_choice_rows == 0, mix_values, 0.0), axis=-1))
    share = chosen / lax.optimization_barrier(jnp.sum(mix_values, axis=-1))
    return (select, share)

def relay_segment_advance(packed):
    travelling_state, expert_choice_rows, router_weight_rows, gain_row, adapter_down_factor, adapter_up_factor, weight_in, weight_out = packed
    values = travelling_state.astype(jnp.float32)
    scale = lax.rsqrt(lax.optimization_barrier(jnp.mean(values * values, axis=-1, keepdims=True)) + 1e-05)
    normed = (values * scale * gain_row.astype(jnp.float32)).astype(jnp.bfloat16)
    flat_normed = normed.reshape(N_EXPERT * TOK_DEV, MODEL_WIDTH)
    low = jnp.dot(flat_normed, adapter_down_factor, preferred_element_type=jnp.float32).astype(jnp.bfloat16)
    adapter = jnp.dot(low, adapter_up_factor, preferred_element_type=jnp.float32).reshape(N_EXPERT, TOK_DEV, MODEL_WIDTH)
    adapted = (values + adapter).astype(jnp.bfloat16)
    select, share = jax.vmap(window_tables)(expert_choice_rows, router_weight_rows)
    slot_rows = jax.vmap(lambda s, n: jnp.dot(s, n, preferred_element_type=jnp.float32))(select, normed).astype(jnp.bfloat16)
    rows = slot_rows.reshape(N_EXPERT * CAP, MODEL_WIDTH)
    joined = jnp.dot(rows, weight_in.reshape(MODEL_WIDTH, 2 * HID), preferred_element_type=jnp.float32)
    gate_part = joined[:, :HID]
    up_part = joined[:, HID:]
    activated = (gate_part * jax.nn.sigmoid(1.702 * gate_part) * (up_part + 1.0)).astype(jnp.bfloat16)
    hid_dev = HID // N_EXPERT
    expert_out = jnp.zeros((N_EXPERT * CAP, MODEL_WIDTH), jnp.float32)
    for block in range(N_EXPERT):
        part_value = jnp.dot(activated[:, block * hid_dev:(block + 1) * hid_dev], weight_out[block * hid_dev:(block + 1) * hid_dev], preferred_element_type=jnp.float32).astype(jnp.bfloat16)
        part_value = lax.optimization_barrier(part_value)
        expert_out = expert_out + part_value.astype(jnp.float32)
    expert_out = expert_out.reshape(N_EXPERT, CAP, MODEL_WIDTH)
    picked = jax.vmap(lambda s, e: jnp.dot(s.astype(jnp.float32).T, e, precision=lax.Precision.HIGHEST))(select, expert_out)
    return (adapted.astype(jnp.float32) + share[..., None] * picked).astype(jnp.bfloat16)

def reference(tokens, segment_norm_scale, expert_choice_table, router_weight_table, adapter_down_weight, adapter_up_weight, expert_gate_up_weight, expert_down_weight):
    travelling_state = tokens.reshape(N_SECTION, N_EXPERT, TOK_DEV, MODEL_WIDTH)
    for hop_index in range(HOPS):
        expert_choice_rows = expert_choice_table[hop_index].reshape(N_SECTION, N_EXPERT, TOK_DEV, TOP)
        router_weight_rows = router_weight_table[hop_index].reshape(N_SECTION, N_EXPERT, TOK_DEV, TOP)
        travelling_state = lax.map(relay_segment_advance, (travelling_state, expert_choice_rows, router_weight_rows, segment_norm_scale, adapter_down_weight, adapter_up_weight, expert_gate_up_weight, expert_down_weight))
        travelling_state = jnp.roll(travelling_state, 1, axis=0)
    return travelling_state.reshape(TOKENS, MODEL_WIDTH)
```

```python
import functools

import jax
import jax.numpy as jnp
from jax import lax
from jax.experimental import pallas as pl
from jax.experimental.pallas import tpu as pltpu
from jax.sharding import PartitionSpec as P

CAP = 48
EPS = 1e-05
NONE_SLOT = 64.0
F32 = jnp.float32
BF16 = jnp.bfloat16
VMEM = pltpu.VMEM
PARAMS = pltpu.CompilerParams(vmem_limit_bytes=40 * 1024 * 1024)

NT = (((1,), (1,)), ((), ()))
TN = (((0,), (0,)), ((), ()))


def dot(a, b, dims=(((1,), (0,)), ((), ()))):
    return lax.dot_general(a, b, dims, preferred_element_type=F32)


def vmem():
    return pl.BlockSpec(memory_space=VMEM)


def hbm():
    return pl.BlockSpec(memory_space=pl.ANY)


def smem():
    return pl.BlockSpec(memory_space=pltpu.SMEM)


def shape(dims, kind=BF16):
    return jax.ShapeDtypeStruct(dims, kind)


def row_scale(rows):
    width = rows.shape[1]
    return lax.rsqrt(jnp.sum(rows * rows, axis=1, keepdims=True) / width + EPS)


def tables_kernel(choice_ref, router_ref, tab_ref):
    hops, top, rows = choice_ref.shape
    before = (
        lax.broadcasted_iota(jnp.int32, (rows, rows), 0) < lax.broadcasted_iota(jnp.int32, (rows, rows), 1)
    ).astype(BF16)
    flags, shares = [], []
    for hop in range(hops):
        hit = (choice_ref[hop] == 0).astype(F32)
        mix = router_ref[hop].astype(F32)
        flags.append(jnp.sum(hit, axis=0, keepdims=True))
        shares.append(jnp.sum(hit * mix, axis=0, keepdims=True) / jnp.sum(mix, axis=0, keepdims=True))
    flags = jnp.concatenate(flags + [jnp.zeros((8 - hops, rows), F32)], axis=0)
    position = dot(flags.astype(BF16), before)
    slots = jnp.where(flags > 0.5, position, NONE_SLOT)
    tab_ref[...] = jnp.concatenate([slots[:hops]] + shares, axis=0)


def tables(choice, router):
    hops, top, rows = choice.shape
    return pl.pallas_call(
        tables_kernel,
        out_shape=shape((2 * hops, rows), F32),
        in_specs=[vmem(), vmem()],
        out_specs=vmem(),
        compiler_params=PARAMS,
        name="tables",
    )(choice, router)


def chosen_rows(slot_row):
    rows = slot_row.shape[1]
    slot = lax.broadcasted_iota(jnp.int32, (CAP, rows), 0).astype(F32)
    return (slot == slot_row).astype(BF16)


def first_rows_kernel(stream_ref, tab_ref, gain_ref, rows_ref):
    rows = dot(chosen_rows(tab_ref[0:1, :]), stream_ref[...], NT)
    rows_ref[...] = (rows * row_scale(rows) * gain_ref[...]).astype(BF16)


def first_rows(stream, tab, gain):
    width = stream.shape[0]
    return pl.pallas_call(
        first_rows_kernel,
        out_shape=shape((CAP, width)),
        in_specs=[vmem(), vmem(), vmem()],
        out_specs=vmem(),
        compiler_params=PARAMS,
        name="first_rows",
    )(stream, tab, gain)


def settled(held_rows, width, expert_out, hop):
    info = held_rows[:, width : width + 16].astype(F32)
    slot = info[:, hop : hop + 1]
    share = info[:, 4 + hop : 5 + hop] + info[:, 8 + hop : 9 + hop]
    lanes = lax.broadcasted_iota(jnp.int32, (held_rows.shape[0], CAP), 1).astype(F32)
    pick = (lanes == slot).astype(BF16)
    fetched = dot(pick, expert_out)
    return (held_rows[:, :width].astype(F32) + share * fetched).astype(BF16), info


def next_rows_kernel(hop, held_ref, expert_ref, gain_ref, rows_ref):
    width = expert_ref.shape[1]
    moved, _ = settled(held_ref[...], width, expert_ref[...], hop)
    moved = moved.astype(F32)
    rows_ref[...] = (moved * row_scale(moved) * gain_ref[...]).astype(BF16)


def next_rows(held, expert_out, gain, hop):
    width = expert_out.shape[1]
    return pl.pallas_call(
        functools.partial(next_rows_kernel, hop),
        grid=(1,),
        out_shape=shape((CAP, width)),
        in_specs=[
            pl.BlockSpec((CAP, held.shape[1]), lambda i: (hop + 1, 0)),
            pl.BlockSpec((CAP, width), lambda i: (0, 0)),
            pl.BlockSpec((1, width), lambda i: (0, 0)),
        ],
        out_specs=pl.BlockSpec((CAP, width), lambda i: (0, 0)),
        compiler_params=PARAMS,
        name="next_rows",
    )(held, expert_out, gain)


def adapt_rows(rows, down_ref, up_ref):
    values = rows.astype(F32)
    low = (dot(rows, down_ref[...]) * row_scale(values)).astype(BF16)
    return (values + dot(low, up_ref[...], NT)).astype(BF16)


def store_held(held_ref, rows, info):
    width = rows.shape[1]
    whole = held_ref.shape[1]
    held_ref[:, :width] = rows
    held_ref[:, width:] = jnp.concatenate(
        [info.astype(BF16), jnp.zeros((rows.shape[0], whole - width - info.shape[1]), BF16)], axis=1
    )


def hold_kernel(stream_ref, tab0_ref, tab1_ref, tab2_ref, tab3_ref, down_ref, up_ref, held_ref):
    tabs = [tab0_ref, tab1_ref, tab2_ref, tab3_ref]
    rows = stream_ref.shape[1]
    slots = [tab[hop : hop + 1, :] for hop, tab in enumerate(tabs)]
    shares = [tab[4 + hop : 5 + hop, :] for hop, tab in enumerate(tabs)]
    high = [share.astype(BF16).astype(F32) for share in shares]
    rest = [share - part for share, part in zip(shares, high)]
    place = lax.broadcasted_iota(jnp.int32, (1, rows), 1)
    last = jnp.zeros((1, rows), F32)
    for hop, slot in enumerate(slots):
        last = jnp.where(slot < CAP, float(hop + 1), last)
    info_rows = jnp.concatenate(
        slots
        + high
        + rest
        + [(place // 8).astype(F32), (place % 8).astype(F32), last, jnp.zeros((1, rows), F32)],
        axis=0,
    ).astype(BF16)
    select = jnp.concatenate([chosen_rows(slot) for slot in slots], axis=0)
    info = dot(select, info_rows, NT)
    picked = dot(select, stream_ref[...], NT).astype(BF16)
    store_held(held_ref, adapt_rows(picked, down_ref, up_ref), info)


def hold(stream, tabs, down, up):
    width = stream.shape[0]
    whole = -(-(width + 16) // 128) * 128
    return pl.pallas_call(
        hold_kernel,
        out_shape=shape((len(tabs) * CAP, whole)),
        in_specs=[vmem()] * (3 + len(tabs)),
        out_specs=vmem(),
        compiler_params=PARAMS,
        name="hold",
    )(stream, *tabs, down, up)


def advance_kernel(hop, held_ref, expert_ref, down_ref, up_ref, out_ref):
    width = expert_ref.shape[1]
    moved, info = settled(held_ref[...], width, expert_ref[...], hop)
    store_held(out_ref, adapt_rows(moved, down_ref, up_ref), info)


def advance(held, expert_out, down, up, hop):
    return pl.pallas_call(
        functools.partial(advance_kernel, hop),
        out_shape=shape(held.shape),
        in_specs=[vmem()] * 4,
        out_specs=vmem(),
        compiler_params=PARAMS,
        name="advance",
    )(held, expert_out, down, up)


def expert_kernel(own_ref, a_ref, b_ref, c_ref, in_ref, out_ref, po_ref, pa_ref, pb_ref, pc_ref, rows, wg, wu, wd, sem):
    copies = [
        pltpu.make_async_copy(in_ref.at[0], wg, sem.at[0]),
        pltpu.make_async_copy(in_ref.at[1], wu, sem.at[1]),
        pltpu.make_async_copy(out_ref, wd, sem.at[2]),
    ]
    for copy in copies:
        copy.start()
    for index, ref in enumerate((own_ref, a_ref, b_ref, c_ref)):
        rows[index * CAP : (index + 1) * CAP, :] = ref[...]
    copies[0].wait()
    gate = dot(rows[...], wg[...], NT)
    copies[1].wait()
    up = dot(rows[...], wu[...], NT)
    activated = (gate * jax.nn.sigmoid(1.702 * gate) * (up + 1.0)).astype(BF16)
    copies[2].wait()
    for index, ref in enumerate((po_ref, pa_ref, pb_ref, pc_ref)):
        ref[...] = dot(activated[index * CAP : (index + 1) * CAP], wd[...]).astype(BF16)


def expert(parts, weight_in, weight_out):
    cap, width = parts[0].shape
    hid = weight_out.shape[0]
    return pl.pallas_call(
        expert_kernel,
        out_shape=[shape((cap, width))] * 4,
        in_specs=[vmem()] * 4 + [hbm(), hbm()],
        out_specs=[vmem()] * 4,
        scratch_shapes=[
            VMEM((4 * cap, width), BF16),
            VMEM((hid, width), BF16),
            VMEM((hid, width), BF16),
            VMEM((hid, width), BF16),
            pltpu.SemaphoreType.DMA((3,)),
        ],
        compiler_params=PARAMS,
        name="expert",
    )(*parts, weight_in, weight_out)


def adapt_stage(stream, down, up, chunk):
    width, rows = stream.shape
    total = jnp.zeros((down.shape[1], rows), F32)
    squares = jnp.zeros((1, rows), F32)
    for at in range(0, width, chunk):
        part = stream[at : at + chunk, :]
        total += dot(down[at : at + chunk, :], part, TN)
        values = part.astype(F32)
        squares += jnp.sum(values * values, axis=0, keepdims=True)
    low = (total * lax.rsqrt(squares / width + EPS)).astype(BF16)
    for at in range(0, width, chunk):
        part = stream[at : at + chunk, :].astype(F32)
        stream[at : at + chunk, :] = (part + dot(up[at : at + chunk, :], low)).astype(BF16)


def fetch_all(pairs, sem):
    copies = [pltpu.make_async_copy(src, dst, sem.at[k]) for k, (src, dst) in enumerate(pairs)]
    for copy in copies:
        copy.start()
    for copy in copies:
        copy.wait()


CHUNK = 576


def bulk_first_kernel(odd_ref, stream_ref, down_ref, up_ref, odown_ref, oup_ref, out_ref, down, up, sem):
    even = odd_ref[0] == 0
    out_ref[...] = stream_ref[...]
    fetch_all([(down_ref, down), (up_ref, up)], sem)
    adapt_stage(out_ref, down, up, CHUNK)

    @pl.when(even)
    def _():
        fetch_all([(odown_ref, down), (oup_ref, up)], sem)
        adapt_stage(out_ref, down, up, CHUNK)


def bulk_second_kernel(odd_ref, stream_ref, rdown_ref, rup_ref, qdown_ref, qup_ref, out_ref, down, up, sem):
    odd = odd_ref[0]
    out_ref[...] = stream_ref[...]
    for step in range(2):

        @pl.when(odd == step)
        def _():
            fetch_all([(rdown_ref, down), (rup_ref, up)], sem)

        @pl.when(odd != step)
        def _():
            fetch_all([(qdown_ref, down), (qup_ref, up)], sem)

        adapt_stage(out_ref, down, up, CHUNK)


def bulk_call(kernel, odd, stream, weights, name):
    scratch = [VMEM(weights[0].shape, BF16), VMEM(weights[1].shape, BF16), pltpu.SemaphoreType.DMA((2,))]
    return pl.pallas_call(
        kernel,
        out_shape=shape(stream.shape),
        in_specs=[smem(), vmem()] + [hbm()] * len(weights),
        out_specs=vmem(),
        scratch_shapes=scratch,
        compiler_params=PARAMS,
        name=name,
    )(odd, stream, *weights)


def bulk_last_kernel(odd_ref, stream_ref, down_ref, up_ref, out_ref, held, down, up, sem, done):
    @pl.when(odd_ref[0] == 1)
    def _():
        fetch_all([(down_ref, down), (up_ref, up), (stream_ref, held)], sem)
        adapt_stage(held, down, up, CHUNK)
        copy = pltpu.make_async_copy(held, out_ref, done)
        copy.start()
        copy.wait()


def bulk_last(odd, stream, down, up):
    return pl.pallas_call(
        bulk_last_kernel,
        out_shape=shape(stream.shape),
        in_specs=[smem(), hbm(), hbm(), hbm()],
        out_specs=hbm(),
        input_output_aliases={1: 0},
        scratch_shapes=[
            VMEM(stream.shape, BF16),
            VMEM(down.shape, BF16),
            VMEM(up.shape, BF16),
            pltpu.SemaphoreType.DMA((3,)),
            pltpu.SemaphoreType.DMA,
        ],
        compiler_params=PARAMS,
        name="bulk_last",
    )(odd, stream, down, up)


def finish_kernel(hop, held_ref, expert_ref, bulk_ref, out_ref):
    width = expert_ref.shape[1]
    moved, info = settled(held_ref[...], width, expert_ref[...], hop)
    count = moved.shape[0]
    rows = bulk_ref.shape[1]
    window = (lax.broadcasted_iota(jnp.int32, (count, 1), 0) // CAP + 1).astype(F32)
    place = jnp.where(info[:, 14:15] == window, info[:, 12:13] * 8.0 + info[:, 13:14], -1.0)
    put = (lax.broadcasted_iota(jnp.int32, (count, rows), 1).astype(F32) == place).astype(BF16)
    covered = jnp.sum(put.astype(F32), axis=0, keepdims=True) > 0.5
    for at in range(0, width, 640):
        size = min(640, width - at)
        back = dot(moved[:, at : at + size], put, TN)
        out_ref[at : at + size, :] = jnp.where(covered, back, bulk_ref[at : at + size, :].astype(F32)).astype(BF16)


def finish(held, expert_out, bulk, hop):
    return pl.pallas_call(
        functools.partial(finish_kernel, hop),
        out_shape=shape(bulk.shape),
        in_specs=[vmem()] * 3,
        out_specs=vmem(),
        compiler_params=PARAMS,
        name="finish",
    )(held, expert_out, bulk)


def along(value, axis, steps):
    count = lax.axis_size(axis)
    return lax.ppermute(value, axis, [(source, (source + steps) % count) for source in range(count)])


def other_core(value):
    count = lax.axis_size("section")
    return lax.ppermute(value, "section", [(source, source ^ 1) for source in range(count)])


AROUND = (1, -1, 2)


def exchange(values):
    return [along(value, "expert", steps) for value, steps in zip(values, AROUND)]


def body(
    tokens,
    segment_norm_scale,
    expert_choice_table,
    router_weight_table,
    adapter_down_weight,
    adapter_up_weight,
    expert_gate_up_weight,
    expert_down_weight,
):
    hops = expert_choice_table.shape[0]
    stream = tokens.T
    gain = segment_norm_scale
    weight_in = jnp.transpose(expert_gate_up_weight[0], (1, 2, 0))
    weight_out = expert_down_weight[0]
    up = adapter_up_weight[0].T
    down = (gain[0][:, None] * adapter_down_weight[0].astype(F32)).astype(BF16)
    odd = (lax.axis_index("section") % 2).astype(jnp.int32).reshape(1)

    tab = tables(jnp.transpose(expert_choice_table, (0, 2, 1)), jnp.transpose(router_weight_table, (0, 2, 1)))
    tabs = [tab] + [along(tab, "section", -hop) for hop in range(1, hops)]
    near = [along(value, "section", -2) for value in (down, up)]
    mate = [other_core(value) for value in (down, up)]
    near_mate = [other_core(value) for value in near]

    slot_rows = first_rows(stream, tab, gain)
    held = hold(stream, tabs, down, up)
    bulk = bulk_call(bulk_first_kernel, odd, stream, [down, up] + mate, "bulk_first")
    bulk = bulk_call(bulk_second_kernel, odd, bulk, near + near_mate, "bulk_second")
    bulk = along(bulk, "section", hops)
    bulk = bulk_last(odd, bulk, *mate)

    for hop in range(hops):
        parts = [slot_rows] + exchange([slot_rows] * 3)
        partial = expert(parts, weight_in, weight_out)
        back = [along(value, "expert", -steps) for value, steps in zip(partial[1:], AROUND)]
        expert_out = partial[0].astype(F32)
        for value in back:
            expert_out = expert_out + value.astype(F32)
        expert_out = along(expert_out.astype(BF16), "section", 1)
        held = along(held, "section", 1)
        if hop + 1 < hops:
            slot_rows = next_rows(held, expert_out, gain, hop)
            held = advance(held, expert_out, down, up, hop)
    return finish(held, expert_out, bulk, hops - 1).T


def solution(mesh):
    return jax.shard_map(
        body,
        mesh=mesh,
        in_specs=(
            P(("section", "expert"), None),
            P("section", None),
            P(None, ("section", "expert"), None),
            P(None, ("section", "expert"), None),
            P("section", None, None),
            P("section", None, None),
            P("section", None, None, "expert"),
            P("section", "expert", None),
        ),
        out_specs=P(("section", "expert"), None),
        check_vma=False,
    )
```

```python
import functools

import jax
import jax.numpy as jnp
from jax import lax
from jax.experimental import pallas as pl
from jax.experimental.pallas import tpu as pltpu
from jax.sharding import PartitionSpec as P

CAP = 48
EPS = 1e-05
NONE_SLOT = 64.0
F32 = jnp.float32
BF16 = jnp.bfloat16
VMEM = pltpu.VMEM
PARAMS = pltpu.CompilerParams(vmem_limit_bytes=40 * 1024 * 1024)
NT = (((1,), (1,)), ((), ()))
TN = (((0,), (0,)), ((), ()))


def dot(a, b, dims=(((1,), (0,)), ((), ()))):
    return lax.dot_general(a, b, dims, preferred_element_type=F32)


def vmem():
    return pl.BlockSpec(memory_space=VMEM)


def hbm():
    return pl.BlockSpec(memory_space=pl.ANY)


def smem():
    return pl.BlockSpec(memory_space=pltpu.SMEM)


def shape(dims, kind=BF16):
    return jax.ShapeDtypeStruct(dims, kind)


def call(kernel, operands, in_specs, out_shape, name, after=(), **options):
    used = len(operands)

    def with_order(*refs):
        kernel(*refs[:used], *refs[used + len(after) :])

    return pl.pallas_call(
        with_order,
        out_shape=out_shape,
        in_specs=list(in_specs) + [hbm()] * len(after),
        compiler_params=PARAMS,
        name=name,
        **options,
    )(*operands, *after)


def row_scale(rows):
    width = rows.shape[1]
    return lax.rsqrt(jnp.sum(rows * rows, axis=1, keepdims=True) / width + EPS)


def tables_kernel(choice_ref, router_ref, tab_ref):
    hops, top, rows = choice_ref.shape
    before = (
        lax.broadcasted_iota(jnp.int32, (rows, rows), 0) < lax.broadcasted_iota(jnp.int32, (rows, rows), 1)
    ).astype(BF16)
    flags, shares = [], []
    for hop in range(hops):
        hit = (choice_ref[hop] == 0).astype(F32)
        mix = router_ref[hop].astype(F32)
        flags.append(jnp.sum(hit, axis=0, keepdims=True))
        shares.append(jnp.sum(hit * mix, axis=0, keepdims=True) / jnp.sum(mix, axis=0, keepdims=True))
    flags = jnp.concatenate(flags + [jnp.zeros((8 - hops, rows), F32)], axis=0)
    position = dot(flags.astype(BF16), before)
    slots = jnp.where(flags > 0.5, position, NONE_SLOT)
    tab_ref[...] = jnp.concatenate([slots[:hops]] + shares, axis=0)


def tables(choice, router):
    hops, top, rows = choice.shape
    return pl.pallas_call(
        tables_kernel,
        out_shape=shape((2 * hops, rows), F32),
        in_specs=[vmem(), vmem()],
        out_specs=vmem(),
        compiler_params=PARAMS,
        name="tables",
    )(choice, router)


def chosen_rows(slot_row):
    rows = slot_row.shape[1]
    slot = lax.broadcasted_iota(jnp.int32, (CAP, rows), 0).astype(F32)
    return (slot == slot_row).astype(BF16)


def settled(held_rows, width, expert_out, hop):
    info = held_rows[:, width : width + 16].astype(F32)
    slot = info[:, hop : hop + 1]
    share = info[:, 4 + hop : 5 + hop] + info[:, 8 + hop : 9 + hop]
    lanes = lax.broadcasted_iota(jnp.int32, (held_rows.shape[0], CAP), 1).astype(F32)
    pick = (lanes == slot).astype(BF16)
    fetched = dot(pick, expert_out)
    return (held_rows[:, :width].astype(F32) + share * fetched).astype(BF16), info


def next_rows_kernel(hop, held_ref, expert_ref, gain_ref, rows_ref):
    width = expert_ref.shape[1]
    moved, _ = settled(held_ref[...], width, expert_ref[...], hop)
    moved = moved.astype(F32)
    rows_ref[...] = (moved * row_scale(moved) * gain_ref[...]).astype(BF16)


def next_rows(held, expert_out, gain, hop, after):
    width = expert_out.shape[1]
    return call(
        functools.partial(next_rows_kernel, hop),
        [held, expert_out, gain],
        [
            pl.BlockSpec((CAP, held.shape[1]), lambda i: (hop + 1, 0)),
            pl.BlockSpec((CAP, width), lambda i: (0, 0)),
            pl.BlockSpec((1, width), lambda i: (0, 0)),
        ],
        shape((CAP, width)),
        "next_rows",
        after,
        grid=(1,),
        out_specs=pl.BlockSpec((CAP, width), lambda i: (0, 0)),
    )


def adapt_rows(rows, factors_ref):
    width = rows.shape[1]
    values = rows.astype(F32)
    low = (dot(rows, factors_ref[:width, :]) * row_scale(values)).astype(BF16)
    return (values + dot(low, factors_ref[width:, :], NT)).astype(BF16)


def store_held(held_ref, rows, info):
    width = rows.shape[1]
    whole = held_ref.shape[1]
    held_ref[:, :width] = rows
    held_ref[:, width:] = jnp.concatenate(
        [info.astype(BF16), jnp.zeros((rows.shape[0], whole - width - info.shape[1]), BF16)], axis=1
    )


def hold_kernel(stream_ref, tab0_ref, tab1_ref, tab2_ref, tab3_ref, factors_ref, gain_ref, rows_ref, held_ref):
    tabs = [tab0_ref, tab1_ref, tab2_ref, tab3_ref]
    rows = stream_ref.shape[1]
    slots = [tab[hop : hop + 1, :] for hop, tab in enumerate(tabs)]
    shares = [tab[4 + hop : 5 + hop, :] for hop, tab in enumerate(tabs)]
    high = [share.astype(BF16).astype(F32) for share in shares]
    rest = [share - part for share, part in zip(shares, high)]
    place = lax.broadcasted_iota(jnp.int32, (1, rows), 1)
    last = jnp.zeros((1, rows), F32)
    for hop, slot in enumerate(slots):
        last = jnp.where(slot < CAP, float(hop + 1), last)
    info_rows = jnp.concatenate(
        slots
        + high
        + rest
        + [(place // 8).astype(F32), (place % 8).astype(F32), last, jnp.zeros((1, rows), F32)],
        axis=0,
    ).astype(BF16)
    select = jnp.concatenate([chosen_rows(slot) for slot in slots], axis=0)
    info = dot(select, info_rows, NT)
    picked = dot(select, stream_ref[...], NT).astype(BF16)
    first = picked[:CAP].astype(F32)
    rows_ref[...] = (first * row_scale(first) * gain_ref[...]).astype(BF16)
    store_held(held_ref, adapt_rows(picked, factors_ref), info)


def hold(stream, tabs, factors, gain):
    width = stream.shape[0]
    whole = -(-(width + 16) // 128) * 128
    return call(
        hold_kernel,
        [stream, *tabs, factors, gain],
        [vmem()] * (3 + len(tabs)),
        [shape((CAP, width)), shape((len(tabs) * CAP, whole))],
        "hold",
        out_specs=[vmem(), vmem()],
    )


def expert_kernel(hop, *refs):
    advance = 3 if hop else 0
    part_refs, (in_ref, out_ref), held_refs = refs[:4], refs[4:6], refs[6 : 6 + advance]
    refs = refs[6 + advance :]
    partial_refs, next_refs = refs[:4], refs[4 : 5 if hop else 4]
    rows, wg, wu, wd, sem = refs[5 if hop else 4 :]
    copies = [
        pltpu.make_async_copy(in_ref.at[0], wg, sem.at[0]),
        pltpu.make_async_copy(in_ref.at[1], wu, sem.at[1]),
        pltpu.make_async_copy(out_ref, wd, sem.at[2]),
    ]
    for copy in copies:
        copy.start()
    for index, ref in enumerate(part_refs):
        rows[index * CAP : (index + 1) * CAP, :] = ref[...]
    if hop:
        held_ref, arrived_ref, factors_ref = held_refs
        moved, info = settled(held_ref[...], arrived_ref.shape[1], arrived_ref[...], hop - 1)
        store_held(next_refs[0], adapt_rows(moved, factors_ref), info)
    copies[0].wait()
    gate = dot(rows[...], wg[...], NT)
    copies[1].wait()
    up = dot(rows[...], wu[...], NT)
    activated = (gate * jax.nn.sigmoid(1.702 * gate) * (up + 1.0)).astype(BF16)
    copies[2].wait()
    for index, ref in enumerate(partial_refs):
        ref[...] = dot(activated[index * CAP : (index + 1) * CAP], wd[...]).astype(BF16)


def expert(hop, parts, weight_in, weight_out, held, after):
    cap, width = parts[0].shape
    hid = weight_out.shape[0]
    outs = [shape((cap, width))] * 4 + ([shape(held[0].shape)] if hop else [])
    return call(
        functools.partial(expert_kernel, hop),
        [*parts, weight_in, weight_out, *held],
        [vmem()] * 4 + [hbm(), hbm()] + [vmem()] * len(held),
        outs,
        "expert",
        after,
        out_specs=[vmem()] * len(outs),
        scratch_shapes=[
            VMEM((4 * cap, width), BF16),
            VMEM((hid, width), BF16),
            VMEM((hid, width), BF16),
            VMEM((hid, width), BF16),
            pltpu.SemaphoreType.DMA((3,)),
        ],
    )


def total_kernel(a_ref, b_ref, c_ref, d_ref, out_ref):
    total = a_ref[...].astype(F32) + b_ref[...].astype(F32) + c_ref[...].astype(F32) + d_ref[...].astype(F32)
    out_ref[...] = total.astype(BF16)


def total(parts, after):
    return call(total_kernel, parts, [vmem()] * 4, shape(parts[0].shape), "total", after, out_specs=vmem())


def adapt_stage(stream, factors, chunk):
    width, rows = stream.shape
    total = jnp.zeros((factors.shape[1], rows), F32)
    squares = jnp.zeros((1, rows), F32)
    for at in range(0, width, chunk):
        part = stream[at : at + chunk, :]
        total += dot(factors[at : at + chunk, :], part, TN)
        values = part.astype(F32)
        squares += jnp.sum(values * values, axis=0, keepdims=True)
    low = (total * lax.rsqrt(squares / width + EPS)).astype(BF16)
    for at in range(0, width, chunk):
        part = stream[at : at + chunk, :].astype(F32)
        stream[at : at + chunk, :] = (part + dot(factors[width + at : width + at + chunk, :], low)).astype(BF16)


def fetch(source, target, sem):
    copy = pltpu.make_async_copy(source, target, sem)
    copy.start()
    copy.wait()


CHUNK = 576
PIECES = (768, 768, 768, 576)
STARTS = (0, 768, 1536, 2304)


def bulk_first_kernel(odd_ref, stream_ref, own_ref, mate_ref, out_ref, factors, sem):
    fetch(own_ref, factors, sem)
    out_ref[...] = stream_ref[...]
    adapt_stage(out_ref, factors, CHUNK)

    @pl.when(odd_ref[0] == 0)
    def _():
        fetch(mate_ref, factors, sem)
        adapt_stage(out_ref, factors, CHUNK)


def bulk_second_kernel(odd_ref, stream_ref, near_ref, near_mate_ref, *rest):
    out_refs, (held, factors, sem) = rest[: len(PIECES)], rest[len(PIECES) :]
    odd = odd_ref[0]
    held[...] = stream_ref[...]
    for step in range(2):

        @pl.when(odd == step)
        def _():
            fetch(near_ref, factors, sem)

        @pl.when(odd != step)
        def _():
            fetch(near_mate_ref, factors, sem)

        adapt_stage(held, factors, CHUNK)
    for ref, at, rows in zip(out_refs, STARTS, PIECES):
        ref[...] = held[at : at + rows, :]


def bulk_first(odd, stream, own, mate, after):
    return call(
        bulk_first_kernel,
        [odd, stream, own, mate],
        [smem(), vmem(), hbm(), hbm()],
        shape(stream.shape),
        "bulk_first",
        after,
        out_specs=vmem(),
        scratch_shapes=[VMEM(own.shape, BF16), pltpu.SemaphoreType.DMA],
    )


def bulk_second(odd, stream, near, near_mate, after):
    return call(
        bulk_second_kernel,
        [odd, stream, near, near_mate],
        [smem(), vmem(), hbm(), hbm()],
        [shape((size, stream.shape[1])) for size in PIECES],
        "bulk_second",
        after,
        out_specs=[vmem()] * len(PIECES),
        scratch_shapes=[VMEM(stream.shape, BF16), VMEM(near.shape, BF16), pltpu.SemaphoreType.DMA],
    )


def release_kernel(piece_ref, out_ref):
    pass


def release(piece, after):
    return call(
        release_kernel,
        [piece],
        [hbm()],
        shape(piece.shape),
        "release",
        after,
        out_specs=hbm(),
        input_output_aliases={0: 0},
    )


def bulk_last_kernel(odd_ref, *refs):
    count = len(PIECES)
    piece_refs, (mate_ref, out_ref, factors, sem) = refs[:count], refs[count:]
    copies = [
        pltpu.make_async_copy(ref, out_ref.at[pl.ds(at, rows), :], sem.at[index])
        for index, (ref, at, rows) in enumerate(zip(piece_refs, STARTS, PIECES))
    ]
    for copy in copies:
        copy.start()
    for copy in copies:
        copy.wait()

    @pl.when(odd_ref[0] == 1)
    def _():
        fetch(mate_ref, factors, sem.at[count])
        adapt_stage(out_ref, factors, CHUNK)


def bulk_last(odd, pieces, mate):
    columns = pieces[0].shape[1]
    return pl.pallas_call(
        bulk_last_kernel,
        out_shape=shape((sum(PIECES), columns)),
        in_specs=[smem()] + [hbm()] * (len(PIECES) + 1),
        out_specs=vmem(),
        scratch_shapes=[VMEM(mate.shape, BF16), pltpu.SemaphoreType.DMA((len(PIECES) + 1,))],
        compiler_params=PARAMS,
        name="bulk_last",
    )(odd, *pieces, mate)


def finish_kernel(hop, held_ref, expert_ref, bulk_ref, out_ref):
    width = expert_ref.shape[1]
    moved, info = settled(held_ref[...], width, expert_ref[...], hop)
    count = moved.shape[0]
    rows = bulk_ref.shape[1]
    window = (lax.broadcasted_iota(jnp.int32, (count, 1), 0) // CAP + 1).astype(F32)
    place = jnp.where(info[:, 14:15] == window, info[:, 12:13] * 8.0 + info[:, 13:14], -1.0)
    put = (lax.broadcasted_iota(jnp.int32, (count, rows), 1).astype(F32) == place).astype(BF16)
    covered = jnp.sum(put.astype(F32), axis=0, keepdims=True) > 0.5
    for at in range(0, width, 640):
        size = min(640, width - at)
        back = dot(moved[:, at : at + size], put, TN)
        out_ref[at : at + size, :] = jnp.where(covered, back, bulk_ref[at : at + size, :].astype(F32)).astype(BF16)


def finish(held, expert_out, bulk, hop):
    return pl.pallas_call(
        functools.partial(finish_kernel, hop),
        out_shape=shape(bulk.shape),
        in_specs=[vmem()] * 3,
        out_specs=vmem(),
        compiler_params=PARAMS,
        name="finish",
    )(held, expert_out, bulk)


def along(value, axis, steps):
    count = lax.axis_size(axis)
    return lax.ppermute(value, axis, [(source, (source + steps) % count) for source in range(count)])


def other_core(value):
    count = lax.axis_size("section")
    return lax.ppermute(value, "section", [(source, source ^ 1) for source in range(count)])


def by_chips(source, steps):
    y, x, core = source // 8, source // 2 % 4, source % 2
    if steps == 1:
        return y * 8 + (x - 1) % 4 * 2 + core
    return (source + 4) % 32


def backwards(value, step):
    pairs = [(source, by_chips(source, 1)) for source in range(32)]
    if step == 1:
        pairs = [(by_chips(source, 1), by_chips(source, 2)) for source in range(32)]
    return lax.ppermute(value, "section", pairs)


AROUND = (1, -1, 2)


def exchange(values):
    return [along(value, "expert", steps) for value, steps in zip(values, AROUND)]


def body(
    tokens,
    segment_norm_scale,
    expert_choice_table,
    router_weight_table,
    adapter_down_weight,
    adapter_up_weight,
    expert_gate_up_weight,
    expert_down_weight,
):
    hops = expert_choice_table.shape[0]
    stream = tokens.T
    gain = segment_norm_scale
    weight_in = jnp.transpose(expert_gate_up_weight[0], (1, 2, 0))
    weight_out = expert_down_weight[0]
    down = (gain[0][:, None] * adapter_down_weight[0].astype(F32)).astype(BF16)
    factors = jnp.concatenate([down, adapter_up_weight[0].T], axis=0)
    odd = (lax.axis_index("section") % 2).astype(jnp.int32).reshape(1)

    tab = tables(jnp.transpose(expert_choice_table, (0, 2, 1)), jnp.transpose(router_weight_table, (0, 2, 1)))
    tabs = [tab] + [along(tab, "section", -hop) for hop in range(1, hops)]

    near = along(release(factors, tabs[1:]), "section", -2)
    slot_rows, held = hold(stream, tabs, factors, gain)
    mate = other_core(factors)
    bulk = bulk_first(odd, stream, factors, mate, [slot_rows])
    expert_out = None
    sent = []

    for hop in range(hops):
        parts = [slot_rows] + exchange([slot_rows] * 3)
        if hop == 0:
            partial = expert(hop, parts, weight_in, weight_out, [], [bulk])
            held = release(held, partial[:1])
        else:
            *partial, held = expert(hop, parts, weight_in, weight_out, [held, expert_out, factors], sent[-1:])
        held = along(held, "section", 1)
        around = [held] if hop == 0 else []
        if hop in (1, 2):
            round_way = backwards(release(round_way, partial[:1]), hop - 1)
            around = [round_way]
        back = [along(value, "expert", -steps) for value, steps in zip(partial[1:], AROUND)]
        summed = total([partial[0]] + back, around)
        expert_out = along(summed, "section", 1)
        ready = []
        if hop == 0:
            near = release(near, [summed])
            *pieces, round_way = bulk_second(odd, bulk, near, other_core(near), [])
            ready = [round_way]
        if hop + 1 < hops:
            sent.append(along(release(pieces[hop], [expert_out]), "section", hops))
            slot_rows = next_rows(held, expert_out, gain, hop, ready)
    bulk = bulk_last(odd, sent + [round_way], mate)
    return finish(held, expert_out, bulk, hops - 1).T


def solution(mesh):
    return jax.shard_map(
        body,
        mesh=mesh,
        in_specs=(
            P(("section", "expert"), None),
            P("section", None),
            P(None, ("section", "expert"), None),
            P(None, ("section", "expert"), None),
            P("section", None, None),
            P("section", None, None),
            P("section", None, None, "expert"),
            P("section", "expert", None),
        ),
        out_specs=P(("section", "expert"), None),
        check_vma=False,
    )
```

```python
import functools

import jax
import jax.numpy as jnp
from jax import lax
from jax.experimental import pallas as pl
from jax.experimental.pallas import tpu as pltpu
from jax.sharding import PartitionSpec as P

CAP = 48
EPS = 1e-05
NONE_SLOT = 64.0
F32 = jnp.float32
BF16 = jnp.bfloat16
VMEM = pltpu.VMEM
PARAMS = pltpu.CompilerParams(vmem_limit_bytes=40 * 1024 * 1024)
NT = (((1,), (1,)), ((), ()))
TN = (((0,), (0,)), ((), ()))


def dot(a, b, dims=(((1,), (0,)), ((), ()))):
    return lax.dot_general(a, b, dims, preferred_element_type=F32)


def vmem():
    return pl.BlockSpec(memory_space=VMEM)


def hbm():
    return pl.BlockSpec(memory_space=pl.ANY)


def smem():
    return pl.BlockSpec(memory_space=pltpu.SMEM)


def shape(dims, kind=BF16):
    return jax.ShapeDtypeStruct(dims, kind)


def call(kernel, operands, in_specs, out_shape, name, after=(), **options):
    used = len(operands)

    def with_order(*refs):
        kernel(*refs[:used], *refs[used + len(after) :])

    return pl.pallas_call(
        with_order,
        out_shape=out_shape,
        in_specs=list(in_specs) + [hbm()] * len(after),
        compiler_params=PARAMS,
        name=name,
        **options,
    )(*operands, *after)


def row_scale(rows):
    width = rows.shape[1]
    return lax.rsqrt(jnp.sum(rows * rows, axis=1, keepdims=True) / width + EPS)


def tables_kernel(choice_ref, router_ref, tab_ref):
    hops, top, rows = choice_ref.shape
    before = (
        lax.broadcasted_iota(jnp.int32, (rows, rows), 0) < lax.broadcasted_iota(jnp.int32, (rows, rows), 1)
    ).astype(BF16)
    flags, shares = [], []
    for hop in range(hops):
        hit = (choice_ref[hop] == 0).astype(F32)
        mix = router_ref[hop].astype(F32)
        flags.append(jnp.sum(hit, axis=0, keepdims=True))
        shares.append(jnp.sum(hit * mix, axis=0, keepdims=True) / jnp.sum(mix, axis=0, keepdims=True))
    flags = jnp.concatenate(flags + [jnp.zeros((8 - hops, rows), F32)], axis=0)
    position = dot(flags.astype(BF16), before)
    slots = jnp.where(flags > 0.5, position, NONE_SLOT)
    tab_ref[...] = jnp.concatenate([slots[:hops]] + shares, axis=0)


def tables(choice, router):
    hops, top, rows = choice.shape
    return pl.pallas_call(
        tables_kernel,
        out_shape=shape((2 * hops, rows), F32),
        in_specs=[vmem(), vmem()],
        out_specs=vmem(),
        compiler_params=PARAMS,
        name="tables",
    )(choice, router)


def chosen_rows(slot_row):
    rows = slot_row.shape[1]
    slot = lax.broadcasted_iota(jnp.int32, (CAP, rows), 0).astype(F32)
    return (slot == slot_row).astype(BF16)


def settled(held_rows, width, expert_out, hop):
    info = held_rows[:, width : width + 16].astype(F32)
    slot = info[:, hop : hop + 1]
    share = info[:, 4 + hop : 5 + hop] + info[:, 8 + hop : 9 + hop]
    lanes = lax.broadcasted_iota(jnp.int32, (held_rows.shape[0], CAP), 1).astype(F32)
    pick = (lanes == slot).astype(BF16)
    fetched = dot(pick, expert_out)
    return (held_rows[:, :width].astype(F32) + share * fetched).astype(BF16), info


def next_rows_kernel(hop, held_ref, expert_ref, gain_ref, rows_ref):
    width = expert_ref.shape[1]
    moved, _ = settled(held_ref[...], width, expert_ref[...], hop)
    moved = moved.astype(F32)
    rows_ref[...] = (moved * row_scale(moved) * gain_ref[...]).astype(BF16)


def next_rows(held, expert_out, gain, hop, after):
    width = expert_out.shape[1]
    return call(
        functools.partial(next_rows_kernel, hop),
        [held, expert_out, gain],
        [
            pl.BlockSpec((CAP, held.shape[1]), lambda i: (hop + 1, 0)),
            pl.BlockSpec((CAP, width), lambda i: (0, 0)),
            pl.BlockSpec((1, width), lambda i: (0, 0)),
        ],
        shape((CAP, width)),
        "next_rows",
        after,
        grid=(1,),
        out_specs=pl.BlockSpec((CAP, width), lambda i: (0, 0)),
    )


def adapt_rows(rows, factors_ref):
    width = rows.shape[1]
    values = rows.astype(F32)
    low = (dot(rows, factors_ref[:width, :]) * row_scale(values)).astype(BF16)
    return (values + dot(low, factors_ref[width:, :], NT)).astype(BF16)


def store_held(held_ref, rows, info):
    width = rows.shape[1]
    whole = held_ref.shape[1]
    held_ref[:, :width] = rows
    held_ref[:, width:] = jnp.concatenate(
        [info.astype(BF16), jnp.zeros((rows.shape[0], whole - width - info.shape[1]), BF16)], axis=1
    )


def hold_kernel(stream_ref, tab0_ref, tab1_ref, tab2_ref, tab3_ref, factors_ref, gain_ref, rows_ref, held_ref):
    tabs = [tab0_ref, tab1_ref, tab2_ref, tab3_ref]
    rows = stream_ref.shape[1]
    slots = [tab[hop : hop + 1, :] for hop, tab in enumerate(tabs)]
    shares = [tab[4 + hop : 5 + hop, :] for hop, tab in enumerate(tabs)]
    high = [share.astype(BF16).astype(F32) for share in shares]
    rest = [share - part for share, part in zip(shares, high)]
    place = lax.broadcasted_iota(jnp.int32, (1, rows), 1)
    last = jnp.zeros((1, rows), F32)
    for hop, slot in enumerate(slots):
        last = jnp.where(slot < CAP, float(hop + 1), last)
    info_rows = jnp.concatenate(
        slots
        + high
        + rest
        + [(place // 8).astype(F32), (place % 8).astype(F32), last, jnp.zeros((1, rows), F32)],
        axis=0,
    ).astype(BF16)
    select = jnp.concatenate([chosen_rows(slot) for slot in slots], axis=0)
    info = dot(select, info_rows, NT)
    picked = dot(select, stream_ref[...], NT).astype(BF16)
    first = picked[:CAP].astype(F32)
    rows_ref[...] = (first * row_scale(first) * gain_ref[...]).astype(BF16)
    store_held(held_ref, adapt_rows(picked, factors_ref), info)


def hold(stream, tabs, factors, gain):
    width = stream.shape[0]
    whole = -(-(width + 16) // 128) * 128
    return call(
        hold_kernel,
        [stream, *tabs, factors, gain],
        [vmem()] * (3 + len(tabs)),
        [shape((CAP, width)), shape((len(tabs) * CAP, whole))],
        "hold",
        out_specs=[vmem(), vmem()],
    )


def expert_kernel(hop, *refs):
    advance = 3 if hop else 0
    part_refs, (in_ref, out_ref), held_refs = refs[:4], refs[4:6], refs[6 : 6 + advance]
    refs = refs[6 + advance :]
    partial_refs, next_refs = refs[:4], refs[4 : 5 if hop else 4]
    rows = refs[5 if hop else 4]
    for index, ref in enumerate(part_refs):
        rows[index * CAP : (index + 1) * CAP, :] = ref[...]
    if hop:
        held_ref, arrived_ref, factors_ref = held_refs
        moved, info = settled(held_ref[...], arrived_ref.shape[1], arrived_ref[...], hop - 1)
        store_held(next_refs[0], adapt_rows(moved, factors_ref), info)
    gate = dot(rows[...], in_ref[0], NT)
    up = dot(rows[...], in_ref[1], NT)
    activated = (gate * jax.nn.sigmoid(1.702 * gate) * (up + 1.0)).astype(BF16)
    for index, ref in enumerate(partial_refs):
        ref[...] = dot(activated[index * CAP : (index + 1) * CAP], out_ref[...]).astype(BF16)


def expert(hop, parts, weight_in, weight_out, held, after):
    cap, width = parts[0].shape
    outs = [shape((cap, width))] * 4 + ([shape(held[0].shape)] if hop else [])
    return call(
        functools.partial(expert_kernel, hop),
        [*parts, weight_in, weight_out, *held],
        [vmem()] * (6 + len(held)),
        outs,
        "expert",
        after,
        out_specs=[vmem()] * len(outs),
        scratch_shapes=[VMEM((4 * cap, width), BF16)],
    )


def total_kernel(a_ref, b_ref, c_ref, d_ref, out_ref):
    total = a_ref[...].astype(F32) + b_ref[...].astype(F32) + c_ref[...].astype(F32) + d_ref[...].astype(F32)
    out_ref[...] = total.astype(BF16)


def total(parts, after):
    return call(total_kernel, parts, [vmem()] * 4, shape(parts[0].shape), "total", after, out_specs=vmem())


def adapt_stage(stream, factors, chunk):
    width, rows = stream.shape
    total = jnp.zeros((factors.shape[1], rows), F32)
    squares = jnp.zeros((1, rows), F32)
    for at in range(0, width, chunk):
        part = stream[at : at + chunk, :]
        total += dot(factors[at : at + chunk, :], part, TN)
        values = part.astype(F32)
        squares += jnp.sum(values * values, axis=0, keepdims=True)
    low = (total * lax.rsqrt(squares / width + EPS)).astype(BF16)
    for at in range(0, width, chunk):
        part = stream[at : at + chunk, :].astype(F32)
        stream[at : at + chunk, :] = (part + dot(factors[width + at : width + at + chunk, :], low)).astype(BF16)


def fetch(source, target, sem):
    copy = pltpu.make_async_copy(source, target, sem)
    copy.start()
    copy.wait()


CHUNK = 576
PIECES = (768, 864, 864, 384)
STARTS = (0, 768, 1632, 2496)


def bulk_first_kernel(odd_ref, stream_ref, own_ref, mate_ref, out_ref, factors, sem):
    fetch(own_ref, factors, sem)
    out_ref[...] = stream_ref[...]
    adapt_stage(out_ref, factors, CHUNK)

    @pl.when(odd_ref[0] == 0)
    def _():
        fetch(mate_ref, factors, sem)
        adapt_stage(out_ref, factors, CHUNK)


def bulk_second_kernel(odd_ref, stream_ref, near_ref, near_mate_ref, *rest):
    out_refs, (held, factors, sem) = rest[: len(PIECES)], rest[len(PIECES) :]
    odd = odd_ref[0]
    held[...] = stream_ref[...]
    for step in range(2):

        @pl.when(odd == step)
        def _():
            fetch(near_ref, factors, sem)

        @pl.when(odd != step)
        def _():
            fetch(near_mate_ref, factors, sem)

        adapt_stage(held, factors, CHUNK)
    for ref, at, rows in zip(out_refs, STARTS, PIECES):
        ref[...] = held[at : at + rows, :]


def bulk_first(odd, stream, own, mate, after):
    return call(
        bulk_first_kernel,
        [odd, stream, own, mate],
        [smem(), vmem(), hbm(), hbm()],
        shape(stream.shape),
        "bulk_first",
        after,
        out_specs=vmem(),
        scratch_shapes=[VMEM(own.shape, BF16), pltpu.SemaphoreType.DMA],
    )


def bulk_second(odd, stream, near, near_mate, after):
    return call(
        bulk_second_kernel,
        [odd, stream, near, near_mate],
        [smem(), vmem(), hbm(), hbm()],
        [shape((size, stream.shape[1])) for size in PIECES],
        "bulk_second",
        after,
        out_specs=[vmem()] * len(PIECES),
        scratch_shapes=[VMEM(stream.shape, BF16), VMEM(near.shape, BF16), pltpu.SemaphoreType.DMA],
    )


def release_kernel(piece_ref, out_ref):
    pass


def release(piece, after):
    return call(
        release_kernel,
        [piece],
        [hbm()],
        shape(piece.shape),
        "release",
        after,
        out_specs=hbm(),
        input_output_aliases={0: 0},
    )


def bulk_last_kernel(odd_ref, *refs):
    count = len(PIECES)
    piece_refs, (mate_ref, out_ref, factors, sem) = refs[:count], refs[count:]
    copies = [
        pltpu.make_async_copy(ref, out_ref.at[pl.ds(at, rows), :], sem.at[index])
        for index, (ref, at, rows) in enumerate(zip(piece_refs, STARTS, PIECES))
    ]
    for copy in copies:
        copy.start()
    for copy in copies:
        copy.wait()

    @pl.when(odd_ref[0] == 1)
    def _():
        fetch(mate_ref, factors, sem.at[count])
        adapt_stage(out_ref, factors, CHUNK)


def bulk_last(odd, pieces, mate):
    columns = pieces[0].shape[1]
    return pl.pallas_call(
        bulk_last_kernel,
        out_shape=shape((sum(PIECES), columns)),
        in_specs=[smem()] + [hbm()] * (len(PIECES) + 1),
        out_specs=vmem(),
        scratch_shapes=[VMEM(mate.shape, BF16), pltpu.SemaphoreType.DMA((len(PIECES) + 1,))],
        compiler_params=PARAMS,
        name="bulk_last",
    )(odd, *pieces, mate)


def finish_kernel(hop, held_ref, expert_ref, bulk_ref, out_ref):
    width = expert_ref.shape[1]
    moved, info = settled(held_ref[...], width, expert_ref[...], hop)
    count = moved.shape[0]
    rows = bulk_ref.shape[1]
    window = (lax.broadcasted_iota(jnp.int32, (count, 1), 0) // CAP + 1).astype(F32)
    place = jnp.where(info[:, 14:15] == window, info[:, 12:13] * 8.0 + info[:, 13:14], -1.0)
    put = (lax.broadcasted_iota(jnp.int32, (count, rows), 1).astype(F32) == place).astype(BF16)
    covered = jnp.sum(put.astype(F32), axis=0, keepdims=True) > 0.5
    for at in range(0, width, 640):
        size = min(640, width - at)
        back = dot(moved[:, at : at + size], put, TN)
        out_ref[at : at + size, :] = jnp.where(covered, back, bulk_ref[at : at + size, :].astype(F32)).astype(BF16)


def finish(held, expert_out, bulk, hop):
    return pl.pallas_call(
        functools.partial(finish_kernel, hop),
        out_shape=shape(bulk.shape),
        in_specs=[vmem()] * 3,
        out_specs=vmem(),
        compiler_params=PARAMS,
        name="finish",
    )(held, expert_out, bulk)


def along(value, axis, steps):
    count = lax.axis_size(axis)
    return lax.ppermute(value, axis, [(source, (source + steps) % count) for source in range(count)])


def other_core(value):
    count = lax.axis_size("section")
    return lax.ppermute(value, "section", [(source, source ^ 1) for source in range(count)])


def by_chips(source, steps):
    y, x, core = source // 8, source // 2 % 4, source % 2
    if steps == 1:
        return y * 8 + (x - 1) % 4 * 2 + core
    return (source + 4) % 32


def backwards(value, step):
    pairs = [(source, by_chips(source, 1)) for source in range(32)]
    if step == 1:
        pairs = [(by_chips(source, 1), by_chips(source, 2)) for source in range(32)]
    return lax.ppermute(value, "section", pairs)


AROUND = (1, -1, 2)


def exchange(values):
    return [along(value, "expert", steps) for value, steps in zip(values, AROUND)]


def body(
    tokens,
    segment_norm_scale,
    expert_choice_table,
    router_weight_table,
    adapter_down_weight,
    adapter_up_weight,
    expert_gate_up_weight,
    expert_down_weight,
):
    hops = expert_choice_table.shape[0]
    stream = tokens.T
    gain = segment_norm_scale
    weight_in = jnp.transpose(expert_gate_up_weight[0], (1, 2, 0))
    weight_out = expert_down_weight[0]
    down = (gain[0][:, None] * adapter_down_weight[0].astype(F32)).astype(BF16)
    factors = jnp.concatenate([down, adapter_up_weight[0].T], axis=0)
    odd = (lax.axis_index("section") % 2).astype(jnp.int32).reshape(1)

    tab = tables(jnp.transpose(expert_choice_table, (0, 2, 1)), jnp.transpose(router_weight_table, (0, 2, 1)))
    tabs = [tab] + [along(tab, "section", -hop) for hop in range(1, hops)]

    near = along(release(factors, tabs[1:]), "section", -2)
    slot_rows, held = hold(stream, tabs, factors, gain)
    mate = other_core(factors)
    bulk = bulk_first(odd, stream, factors, mate, [slot_rows])
    expert_out = None
    sent = []

    for hop in range(hops):
        parts = [slot_rows] + exchange([slot_rows] * 3)
        if hop == 0:
            partial = expert(hop, parts, weight_in, weight_out, [], [bulk])
            held = release(held, partial[:1])
        else:
            *partial, held = expert(hop, parts, weight_in, weight_out, [held, expert_out, factors], sent[-1:])
        held = along(held, "section", 1)
        around = [held] if hop == 0 else []
        if hop in (1, 2):
            round_way = backwards(release(round_way, partial[:1]), hop - 1)
            around = [round_way]
        back = [along(value, "expert", -steps) for value, steps in zip(partial[1:], AROUND)]
        summed = total([partial[0]] + back, around)
        expert_out = along(summed, "section", 1)
        ready = []
        if hop == 0:
            near = release(near, [summed])
            *pieces, round_way = bulk_second(odd, bulk, near, other_core(near), [])
            ready = [round_way]
        if hop + 1 < hops:
            sent.append(along(release(pieces[hop], [expert_out]), "section", hops))
            slot_rows = next_rows(held, expert_out, gain, hop, ready)
    bulk = bulk_last(odd, sent + [round_way], mate)
    return finish(held, expert_out, bulk, hops - 1).T


def solution(mesh):
    return jax.shard_map(
        body,
        mesh=mesh,
        in_specs=(
            P(("section", "expert"), None),
            P("section", None),
            P(None, ("section", "expert"), None),
            P(None, ("section", "expert"), None),
            P("section", None, None),
            P("section", None, None),
            P("section", None, None, "expert"),
            P("section", "expert", None),
        ),
        out_specs=P(("section", "expert"), None),
        check_vma=False,
    )
```

```python
import functools

import jax
import jax.numpy as jnp
from jax import lax
from jax.experimental import pallas as pl
from jax.experimental.pallas import tpu as pltpu
from jax.sharding import PartitionSpec as P

CAP = 48
EPS = 1e-05
NONE_SLOT = 64.0
F32 = jnp.float32
BF16 = jnp.bfloat16
VMEM = pltpu.VMEM
PARAMS = pltpu.CompilerParams(vmem_limit_bytes=40 * 1024 * 1024)
NT = (((1,), (1,)), ((), ()))
TN = (((0,), (0,)), ((), ()))


def dot(a, b, dims=(((1,), (0,)), ((), ()))):
    return lax.dot_general(a, b, dims, preferred_element_type=F32)


def vmem():
    return pl.BlockSpec(memory_space=VMEM)


def hbm():
    return pl.BlockSpec(memory_space=pl.ANY)


def smem():
    return pl.BlockSpec(memory_space=pltpu.SMEM)


def shape(dims, kind=BF16):
    return jax.ShapeDtypeStruct(dims, kind)


def call(kernel, operands, in_specs, out_shape, name, after=(), **options):
    used = len(operands)

    def with_order(*refs):
        kernel(*refs[:used], *refs[used + len(after) :])

    return pl.pallas_call(
        with_order,
        out_shape=out_shape,
        in_specs=list(in_specs) + [hbm()] * len(after),
        compiler_params=PARAMS,
        name=name,
        **options,
    )(*operands, *after)


def row_scale(rows):
    width = rows.shape[1]
    return lax.rsqrt(jnp.sum(rows * rows, axis=1, keepdims=True) / width + EPS)


def tables_kernel(choice_ref, router_ref, gain_ref, tab_ref, gain_out_ref):
    gain_out_ref[...] = gain_ref[...]
    hops, top, rows = choice_ref.shape
    before = (
        lax.broadcasted_iota(jnp.int32, (rows, rows), 0) < lax.broadcasted_iota(jnp.int32, (rows, rows), 1)
    ).astype(BF16)
    flags, shares = [], []
    for hop in range(hops):
        hit = (choice_ref[hop] == 0).astype(F32)
        mix = router_ref[hop].astype(F32)
        flags.append(jnp.sum(hit, axis=0, keepdims=True))
        shares.append(jnp.sum(hit * mix, axis=0, keepdims=True) / jnp.sum(mix, axis=0, keepdims=True))
    flags = jnp.concatenate(flags + [jnp.zeros((8 - hops, rows), F32)], axis=0)
    position = dot(flags.astype(BF16), before)
    slots = jnp.where(flags > 0.5, position, NONE_SLOT)
    tab_ref[...] = jnp.concatenate([slots[:hops]] + shares, axis=0)


def tables(choice, router, gain):
    hops, top, rows = choice.shape
    return pl.pallas_call(
        tables_kernel,
        out_shape=[shape((2 * hops, rows), F32), shape(gain.shape, F32)],
        in_specs=[vmem()] * 3,
        out_specs=[vmem()] * 2,
        compiler_params=PARAMS,
        name="tables",
    )(choice, router, gain)


def chosen_rows(slot_row):
    rows = slot_row.shape[1]
    slot = lax.broadcasted_iota(jnp.int32, (CAP, rows), 0).astype(F32)
    return (slot == slot_row).astype(BF16)


def settled(held_rows, width, expert_out, hop):
    info = held_rows[:, width : width + 16].astype(F32)
    slot = info[:, hop : hop + 1]
    share = info[:, 4 + hop : 5 + hop] + info[:, 8 + hop : 9 + hop]
    lanes = lax.broadcasted_iota(jnp.int32, (held_rows.shape[0], CAP), 1).astype(F32)
    pick = (lanes == slot).astype(BF16)
    fetched = dot(pick, expert_out)
    return (held_rows[:, :width].astype(F32) + share * fetched).astype(BF16), info


def next_rows_kernel(hop, held_ref, expert_ref, gain_ref, rows_ref):
    width = expert_ref.shape[1]
    moved, _ = settled(held_ref[...], width, expert_ref[...], hop)
    moved = moved.astype(F32)
    rows_ref[...] = (moved * row_scale(moved) * gain_ref[...]).astype(BF16)


def next_rows(held, expert_out, gain, hop, after):
    width = expert_out.shape[1]
    return call(
        functools.partial(next_rows_kernel, hop),
        [held, expert_out, gain],
        [
            pl.BlockSpec((CAP, held.shape[1]), lambda i: (hop + 1, 0)),
            pl.BlockSpec((CAP, width), lambda i: (0, 0)),
            pl.BlockSpec((1, width), lambda i: (0, 0)),
        ],
        shape((CAP, width)),
        "next_rows",
        after,
        grid=(1,),
        out_specs=pl.BlockSpec((CAP, width), lambda i: (0, 0)),
    )


def adapt_rows(rows, factors_ref):
    width = rows.shape[1]
    values = rows.astype(F32)
    low = (dot(rows, factors_ref[:width, :]) * row_scale(values)).astype(BF16)
    return (values + dot(low, factors_ref[width:, :], NT)).astype(BF16)


def store_held(held_ref, rows, info):
    width = rows.shape[1]
    whole = held_ref.shape[1]
    held_ref[:, :width] = rows
    held_ref[:, width:] = jnp.concatenate(
        [info.astype(BF16), jnp.zeros((rows.shape[0], whole - width - info.shape[1]), BF16)], axis=1
    )


def hold_kernel(stream_ref, tab0_ref, tab1_ref, tab2_ref, tab3_ref, factors_ref, gain_ref, rows_ref, held_ref):
    tabs = [tab0_ref, tab1_ref, tab2_ref, tab3_ref]
    rows = stream_ref.shape[1]
    slots = [tab[hop : hop + 1, :] for hop, tab in enumerate(tabs)]
    shares = [tab[4 + hop : 5 + hop, :] for hop, tab in enumerate(tabs)]
    high = [share.astype(BF16).astype(F32) for share in shares]
    rest = [share - part for share, part in zip(shares, high)]
    place = lax.broadcasted_iota(jnp.int32, (1, rows), 1)
    last = jnp.zeros((1, rows), F32)
    for hop, slot in enumerate(slots):
        last = jnp.where(slot < CAP, float(hop + 1), last)
    info_rows = jnp.concatenate(
        slots
        + high
        + rest
        + [(place // 8).astype(F32), (place % 8).astype(F32), last, jnp.zeros((1, rows), F32)],
        axis=0,
    ).astype(BF16)
    select = jnp.concatenate([chosen_rows(slot) for slot in slots], axis=0)
    info = dot(select, info_rows, NT)
    picked = dot(select, stream_ref[...], NT).astype(BF16)
    first = picked[:CAP].astype(F32)
    rows_ref[...] = (first * row_scale(first) * gain_ref[...]).astype(BF16)
    store_held(held_ref, adapt_rows(picked, factors_ref), info)


def hold(stream, tabs, factors, gain):
    width = stream.shape[0]
    whole = -(-(width + 16) // 128) * 128
    return call(
        hold_kernel,
        [stream, *tabs, factors, gain],
        [vmem()] * (3 + len(tabs)),
        [shape((CAP, width)), shape((len(tabs) * CAP, whole))],
        "hold",
        out_specs=[vmem(), vmem()],
    )


def expert_kernel(hop, *refs):
    advance = 3 if hop else 0
    part_refs, (in_ref, out_ref), held_refs = refs[:4], refs[4:6], refs[6 : 6 + advance]
    refs = refs[6 + advance :]
    partial_refs, next_refs = refs[:4], refs[4 : 5 if hop else 4]
    rows = refs[5 if hop else 4]
    for index, ref in enumerate(part_refs):
        rows[index * CAP : (index + 1) * CAP, :] = ref[...]
    if hop:
        held_ref, arrived_ref, factors_ref = held_refs
        moved, info = settled(held_ref[...], arrived_ref.shape[1], arrived_ref[...], hop - 1)
        store_held(next_refs[0], adapt_rows(moved, factors_ref), info)
    gate = dot(rows[...], in_ref[0], NT)
    up = dot(rows[...], in_ref[1], NT)
    activated = (gate * jax.nn.sigmoid(1.702 * gate) * (up + 1.0)).astype(BF16)
    for index, ref in enumerate(partial_refs):
        ref[...] = dot(activated[index * CAP : (index + 1) * CAP], out_ref[...]).astype(BF16)


def expert(hop, parts, weight_in, weight_out, held, after):
    cap, width = parts[0].shape
    outs = [shape((cap, width))] * 4 + ([shape(held[0].shape)] if hop else [])
    return call(
        functools.partial(expert_kernel, hop),
        [*parts, weight_in, weight_out, *held],
        [vmem()] * (6 + len(held)),
        outs,
        "expert",
        after,
        out_specs=[vmem()] * len(outs),
        scratch_shapes=[VMEM((4 * cap, width), BF16)],
    )


def total_kernel(a_ref, b_ref, c_ref, d_ref, out_ref):
    total = a_ref[...].astype(F32) + b_ref[...].astype(F32) + c_ref[...].astype(F32) + d_ref[...].astype(F32)
    out_ref[...] = total.astype(BF16)


def total(parts, after):
    return call(total_kernel, parts, [vmem()] * 4, shape(parts[0].shape), "total", after, out_specs=vmem())


def adapt_stage(stream, factors, chunk):
    width, rows = stream.shape
    total = jnp.zeros((factors.shape[1], rows), F32)
    squares = jnp.zeros((1, rows), F32)
    for at in range(0, width, chunk):
        part = stream[at : at + chunk, :]
        total += dot(factors[at : at + chunk, :], part, TN)
        values = part.astype(F32)
        squares += jnp.sum(values * values, axis=0, keepdims=True)
    low = (total * lax.rsqrt(squares / width + EPS)).astype(BF16)
    for at in range(0, width, chunk):
        part = stream[at : at + chunk, :].astype(F32)
        stream[at : at + chunk, :] = (part + dot(factors[width + at : width + at + chunk, :], low)).astype(BF16)


def fetch(source, target, sem):
    copy = pltpu.make_async_copy(source, target, sem)
    copy.start()
    copy.wait()


CHUNK = 576
PIECES = (768, 864, 864, 384)
STARTS = (0, 768, 1632, 2496)


def bulk_first_kernel(odd_ref, stream_ref, own_ref, mate_ref, out_ref, factors, sem):
    fetch(own_ref, factors, sem)
    out_ref[...] = stream_ref[...]
    adapt_stage(out_ref, factors, CHUNK)

    @pl.when(odd_ref[0] == 0)
    def _():
        fetch(mate_ref, factors, sem)
        adapt_stage(out_ref, factors, CHUNK)


def bulk_second_kernel(odd_ref, stream_ref, near_ref, near_mate_ref, *rest):
    out_refs, (held, factors, sem) = rest[: len(PIECES)], rest[len(PIECES) :]
    odd = odd_ref[0]
    held[...] = stream_ref[...]
    for step in range(2):

        @pl.when(odd == step)
        def _():
            fetch(near_ref, factors, sem)

        @pl.when(odd != step)
        def _():
            fetch(near_mate_ref, factors, sem)

        adapt_stage(held, factors, CHUNK)
    for ref, at, rows in zip(out_refs, STARTS, PIECES):
        ref[...] = held[at : at + rows, :]


def bulk_first(odd, stream, own, mate, after):
    return call(
        bulk_first_kernel,
        [odd, stream, own, mate],
        [smem(), vmem(), hbm(), hbm()],
        shape(stream.shape),
        "bulk_first",
        after,
        out_specs=vmem(),
        scratch_shapes=[VMEM(own.shape, BF16), pltpu.SemaphoreType.DMA],
    )


def bulk_second(odd, stream, near, near_mate, after):
    return call(
        bulk_second_kernel,
        [odd, stream, near, near_mate],
        [smem(), vmem(), hbm(), hbm()],
        [shape((size, stream.shape[1])) for size in PIECES],
        "bulk_second",
        after,
        out_specs=[vmem()] * len(PIECES),
        scratch_shapes=[VMEM(stream.shape, BF16), VMEM(near.shape, BF16), pltpu.SemaphoreType.DMA],
    )


def release_kernel(piece_ref, out_ref):
    pass


def release(piece, after):
    return call(
        release_kernel,
        [piece],
        [hbm()],
        shape(piece.shape),
        "release",
        after,
        out_specs=hbm(),
        input_output_aliases={0: 0},
    )


def bulk_last_kernel(odd_ref, *refs):
    count = len(PIECES)
    piece_refs, (mate_ref, out_ref, factors, sem) = refs[:count], refs[count:]
    copies = [
        pltpu.make_async_copy(ref, out_ref.at[pl.ds(at, rows), :], sem.at[index])
        for index, (ref, at, rows) in enumerate(zip(piece_refs, STARTS, PIECES))
    ]
    for copy in copies:
        copy.start()
    for copy in copies:
        copy.wait()

    @pl.when(odd_ref[0] == 1)
    def _():
        fetch(mate_ref, factors, sem.at[count])
        adapt_stage(out_ref, factors, CHUNK)


def bulk_last(odd, pieces, mate):
    columns = pieces[0].shape[1]
    return pl.pallas_call(
        bulk_last_kernel,
        out_shape=shape((sum(PIECES), columns)),
        in_specs=[smem()] + [hbm()] * (len(PIECES) + 1),
        out_specs=vmem(),
        scratch_shapes=[VMEM(mate.shape, BF16), pltpu.SemaphoreType.DMA((len(PIECES) + 1,))],
        compiler_params=PARAMS,
        name="bulk_last",
    )(odd, *pieces, mate)


def finish_kernel(hop, held_ref, expert_ref, bulk_ref, out_ref):
    width = expert_ref.shape[1]
    moved, info = settled(held_ref[...], width, expert_ref[...], hop)
    count = moved.shape[0]
    rows = bulk_ref.shape[1]
    window = (lax.broadcasted_iota(jnp.int32, (count, 1), 0) // CAP + 1).astype(F32)
    place = jnp.where(info[:, 14:15] == window, info[:, 12:13] * 8.0 + info[:, 13:14], -1.0)
    put = (lax.broadcasted_iota(jnp.int32, (count, rows), 1).astype(F32) == place).astype(BF16)
    covered = jnp.sum(put.astype(F32), axis=0, keepdims=True) > 0.5
    for at in range(0, width, 640):
        size = min(640, width - at)
        back = dot(moved[:, at : at + size], put, TN)
        out_ref[at : at + size, :] = jnp.where(covered, back, bulk_ref[at : at + size, :].astype(F32)).astype(BF16)


def finish(held, expert_out, bulk, hop):
    return pl.pallas_call(
        functools.partial(finish_kernel, hop),
        out_shape=shape(bulk.shape),
        in_specs=[vmem()] * 3,
        out_specs=vmem(),
        compiler_params=PARAMS,
        name="finish",
    )(held, expert_out, bulk)


def along(value, axis, steps):
    count = lax.axis_size(axis)
    return lax.ppermute(value, axis, [(source, (source + steps) % count) for source in range(count)])


def other_core(value):
    count = lax.axis_size("section")
    return lax.ppermute(value, "section", [(source, source ^ 1) for source in range(count)])


def by_chips(source, steps):
    y, x, core = source // 8, source // 2 % 4, source % 2
    if steps == 1:
        return y * 8 + (x - 1) % 4 * 2 + core
    return (source + 4) % 32


def backwards(value, step):
    pairs = [(source, by_chips(source, 1)) for source in range(32)]
    if step == 1:
        pairs = [(by_chips(source, 1), by_chips(source, 2)) for source in range(32)]
    return lax.ppermute(value, "section", pairs)


AROUND = (1, -1, 2)


def exchange(values):
    return [along(value, "expert", steps) for value, steps in zip(values, AROUND)]


def body(
    tokens,
    segment_norm_scale,
    expert_choice_table,
    router_weight_table,
    adapter_down_weight,
    adapter_up_weight,
    expert_gate_up_weight,
    expert_down_weight,
):
    hops = expert_choice_table.shape[0]
    stream = tokens.T
    gain = segment_norm_scale
    weight_in = jnp.transpose(expert_gate_up_weight[0], (1, 2, 0))
    weight_out = expert_down_weight[0]
    choice, router = jnp.transpose(expert_choice_table, (0, 2, 1)), jnp.transpose(router_weight_table, (0, 2, 1))
    tab, gain = tables(choice, router, gain)
    down = (gain[0][:, None] * adapter_down_weight[0].astype(F32)).astype(BF16)
    factors = jnp.concatenate([down, adapter_up_weight[0].T], axis=0)
    odd = (lax.axis_index("section") % 2).astype(jnp.int32).reshape(1)

    tabs = [tab] + [along(tab, "section", -hop) for hop in range(1, hops)]

    later = release(factors, tabs[1:])
    near = along(later, "section", -2)
    slot_rows, held = hold(stream, tabs, factors, gain)
    mate = other_core(later)
    bulk = bulk_first(odd, stream, factors, mate, [slot_rows])
    expert_out = None
    sent = []

    for hop in range(hops):
        parts = [slot_rows] + exchange([slot_rows] * 3)
        if hop == 0:
            partial = expert(hop, parts, weight_in, weight_out, [], [bulk])
            held = release(held, partial[:1])
        else:
            *partial, held = expert(hop, parts, weight_in, weight_out, [held, expert_out, factors], sent[-1:])
        held = along(held, "section", 1)
        around = [held] if hop == 0 else []
        if hop in (1, 2):
            round_way = backwards(release(round_way, partial[:1]), hop - 1)
            around = [round_way]
        back = [along(value, "expert", -steps) for value, steps in zip(partial[1:], AROUND)]
        summed = total([partial[0]] + back, around)
        expert_out = along(summed, "section", 1)
        ready = []
        if hop == 0:
            near = release(near, [summed])
            *pieces, round_way = bulk_second(odd, bulk, near, other_core(near), [])
            ready = [round_way]
        if hop + 1 < hops:
            sent.append(along(release(pieces[hop], [expert_out]), "section", hops))
            slot_rows = next_rows(held, expert_out, gain, hop, ready)
    bulk = bulk_last(odd, sent + [round_way], mate)
    return finish(held, expert_out, bulk, hops - 1).T


def solution(mesh):
    return jax.shard_map(
        body,
        mesh=mesh,
        in_specs=(
            P(("section", "expert"), None),
            P("section", None),
            P(None, ("section", "expert"), None),
            P(None, ("section", "expert"), None),
            P("section", None, None),
            P("section", None, None),
            P("section", None, None, "expert"),
            P("section", "expert", None),
        ),
        out_specs=P(("section", "expert"), None),
        check_vma=False,
    )
```
